32 devices in a mesh: wide: 8 (over z, y), sub: 4 (over x, core).
Axes of the slice: x: 2, y: 2, z: 4, core: 2. Of those that a mesh axis runs over, the one named last changes fastest.
Arguments:
- embeddings: bfloat16 [4096, 1024], P(('wide', 'sub'))
- cluster_ids: int32 [4096], P(('wide', 'sub')), may hold values from 0 to 383, as said below
Outputs:
- nearest: float32 [4096], P(('wide', 'sub'))
The draws below stay inside these ranges and needn't reach their ends.
Inputs may be any that keep to these rules, and one draw needn't show every extreme that they name: `cluster_ids`: cluster c belongs to owner c // 48 (an index along wide). Among the 128 documents of one device, at most 32 lie in clusters of one owner; in every draw some owner has exactly 32 such documents from every device. A cluster holds at most 44 documents, and some cluster holds exactly that many.
All inputs are finite; a program needn't handle non-finite values.
Results may differ from the reference program's by a relative error of at most 0.00047.
Values may be sent and summed in bfloat16 or wider, within the bound.
A program may use at most 64 MiB of HBM per device.

```python
import jax
import jax.numpy as jnp
from jax import lax

D = 1024
DOC_DEV = 128
CL_DEV = 48
CAP = 32
CLUSTER_MOST = 44
N_WIDE = 8
N_SUB = 4


def layout(key):
    key_weight, key_forced, key_raw, key_shuffle, key_tie, key_sizes = jax.random.split(key, 6)
    devices = N_WIDE * N_SUB
    total_slots = N_WIDE * CAP
    total_docs = DOC_DEV * devices
    slot_owner = jnp.arange(total_slots, dtype=jnp.int32) // CAP
    weight = jax.random.randint(key_weight, (N_WIDE,), 1, 9)
    forced = jax.random.randint(key_forced, (), 0, N_WIDE)
    raw = jax.random.randint(key_raw, (devices, total_slots), 0, 2 ** 14)
    scores = raw * weight[slot_owner][None, :] * 2048 + jnp.arange(total_slots, dtype=jnp.int32)[None, :]
    scores = scores + jnp.where(slot_owner == forced, 2 ** 29, 0)[None, :]
    scores = scores + jnp.where(jnp.arange(total_slots, dtype=jnp.int32) == total_slots - 1, 2 ** 29, 0)[None, :]
    _, chosen = lax.top_k(scores, DOC_DEV)
    chosen = jax.random.permutation(key_shuffle, chosen, axis=1, independent=True)
    doc_owner = (chosen // CAP).reshape(-1).astype(jnp.int32)
    tie_break = jax.random.permutation(key_tie, total_docs).astype(jnp.int32)
    sorted_pos = jnp.argsort(doc_owner * total_docs + tie_break).astype(jnp.int32)
    counts = jnp.zeros((N_WIDE,), jnp.int32).at[doc_owner].add(1)
    owner_start = jnp.cumsum(counts) - counts
    slot_rank = jnp.zeros((total_docs,), jnp.int32).at[sorted_pos].set(jnp.arange(total_docs, dtype=jnp.int32) - owner_start[doc_owner[sorted_pos]])
    back_rank = counts[doc_owner] - 1 - slot_rank
    sizes = jax.random.randint(key_sizes, (N_WIDE, CL_DEV), CLUSTER_MOST // 2, CLUSTER_MOST + 1)
    sizes = sizes.at[:, 0].set(CLUSTER_MOST)
    bounds = jnp.cumsum(sizes, axis=1)
    local = CL_DEV - 1 - jnp.sum((back_rank[:, None] >= bounds[doc_owner]).astype(jnp.int32), axis=1)
    return (doc_owner * CL_DEV + local).astype(jnp.int32)


def draw_cluster_ids(key, part):
    return layout(key)


def draw_embeddings(key, part):
    clusters = layout(key)
    key = jax.random.fold_in(key, 11)
    key_center, key_noise, key_spread, key_scale = jax.random.split(key, 4)
    total_docs = DOC_DEV * N_WIDE * N_SUB
    centers = jax.random.normal(key_center, (CL_DEV * N_WIDE, D), jnp.float32)
    noise = jax.random.normal(key_noise, (total_docs, D), jnp.float32)
    spread = jnp.exp(jax.random.uniform(key_spread, (total_docs, 1), jnp.float32, jnp.log(0.2), jnp.log(2.0)))
    scale = jnp.exp(jax.random.uniform(key_scale, (total_docs, 1), jnp.float32, jnp.log(0.5), jnp.log(4.0)))
    return ((centers[clusters] + spread * noise) * scale).astype(jnp.bfloat16)


def setup_inputs(seed: int = 0) -> dict:
    seeds = jax.random.split(jax.random.key(seed), 3)
    embeddings = draw_embeddings(jax.random.fold_in(seeds[2], 71), 0)
    cluster_ids = draw_cluster_ids(jax.random.fold_in(seeds[2], 71), 0)
    return {"embeddings": embeddings, "cluster_ids": cluster_ids}


def reference(embeddings, cluster_ids):
    values = embeddings.astype(jnp.float32)
    unit_rows = (values * lax.rsqrt(lax.optimization_barrier(jnp.sum(values * values, axis=1, keepdims=True)) + 1e-06)).astype(jnp.bfloat16)
    total_docs = unit_rows.shape[0]
    sorted_index = jnp.argsort(cluster_ids, stable=True).astype(jnp.int32)
    padded_rows = jnp.concatenate([jnp.zeros((CLUSTER_MOST, D), unit_rows.dtype), unit_rows[sorted_index]], axis=0)
    labels = jnp.concatenate([jnp.full((CLUSTER_MOST,), -1, jnp.int32), cluster_ids[sorted_index].astype(jnp.int32)])
    places = jnp.concatenate([jnp.full((CLUSTER_MOST,), -1, jnp.int32), sorted_index])

    def block_max(first_row):
        query_rows = lax.dynamic_slice_in_dim(padded_rows, first_row + CLUSTER_MOST, 128, 0)
        query_labels = lax.dynamic_slice_in_dim(labels, first_row + CLUSTER_MOST, 128, 0)
        query_places = lax.dynamic_slice_in_dim(places, first_row + CLUSTER_MOST, 128, 0)
        key_rows = lax.dynamic_slice_in_dim(padded_rows, first_row, CLUSTER_MOST + 128, 0)
        key_labels = lax.dynamic_slice_in_dim(labels, first_row, CLUSTER_MOST + 128, 0)
        key_places = lax.dynamic_slice_in_dim(places, first_row, CLUSTER_MOST + 128, 0)
        scores = jnp.dot(query_rows, key_rows.T, preferred_element_type=jnp.float32)
        allowed = (query_labels[:, None] == key_labels[None, :]) & (key_places[None, :] < query_places[:, None])
        return lax.optimization_barrier(jnp.max(jnp.where(allowed, scores, jnp.float32(-1.0)), axis=1))
    starts = jnp.arange(total_docs // 128, dtype=jnp.int32) * 128
    nearest_sorted = lax.map(block_max, starts).reshape(-1)
    return jnp.zeros((total_docs,), jnp.float32).at[sorted_index].set(nearest_sorted)
```

```python
import functools

import jax
import jax.numpy as jnp
from jax import lax
from jax.experimental import pallas as pl
from jax.experimental.pallas import tpu as pltpu
from jax.sharding import PartitionSpec as P

CL_DEV = 48
EPSILON = 1e-06
META = 128
MESH = pl.DeviceIdType.MESH


def raw_scores(query_rows, key_rows):
    return lax.dot_general(
        query_rows, key_rows, (((1,), (1,)), ((), ())), preferred_element_type=jnp.float32
    )


def flip(index, mask, count):
    result, bit = 0, 1
    while bit < count:
        digit = lax.rem(lax.div(index, bit), 2)
        result = result + (1 - digit if mask & bit else digit) * bit
        bit *= 2
    return result


def kernel(wide, cap, emb_ref, ids_ref, out_ref, send, keys, best, answers, sems, back_sems):
    docs, width = emb_ref.shape
    w, s = lax.axis_index("wide"), lax.axis_index("sub")
    group = 4 * cap
    peers = {k: flip(w, k, wide) for k in range(wide)}
    x_peer, core_peer = flip(s, 2, 4), flip(s, 1, 4)

    barrier = pltpu.get_barrier_semaphore()
    for k in range(1, wide):
        pl.semaphore_signal(barrier, inc=1, device_id=(peers[k], s), device_id_type=MESH)
    for t in (x_peer, core_peer):
        pl.semaphore_signal(barrier, inc=1, device_id=(w, t), device_id_type=MESH)

    ids = ids_ref[...]
    owner_row = lax.broadcasted_iota(jnp.int32, (wide, docs), 0)
    own = (ids >= owner_row * CL_DEV) & (ids < owner_row * CL_DEV + CL_DEV)
    ones = jnp.where(own, 1.0, 0.0)
    earlier = lax.broadcasted_iota(jnp.int32, (docs, docs), 0) < lax.broadcasted_iota(
        jnp.int32, (docs, docs), 1
    )
    ranks = jnp.dot(
        ones.astype(jnp.bfloat16),
        jnp.where(earlier, 1.0, 0.0).astype(jnp.bfloat16),
        preferred_element_type=jnp.float32,
    )
    rank = jnp.sum(ones * ranks, axis=0, keepdims=True).astype(jnp.int32)
    owner = jnp.sum(jnp.where(own, owner_row, 0), axis=0, keepdims=True)
    slot = owner * cap + rank
    local = ids - owner * CL_DEV

    values = emb_ref[...].astype(jnp.float32)
    unit = (
        values * lax.rsqrt(jnp.sum(values * values, axis=1, keepdims=True) + EPSILON)
    ).astype(jnp.bfloat16)
    pick = jnp.where(
        lax.broadcasted_iota(jnp.int32, (wide * cap, docs), 0) == slot, 1.0, 0.0
    ).astype(jnp.bfloat16)
    labels = jnp.where(
        lax.broadcasted_iota(jnp.int32, (META, docs), 0) == local, 1.0, 0.0
    ).astype(jnp.bfloat16)
    send[:, :width] = jnp.dot(pick, unit, preferred_element_type=jnp.float32).astype(jnp.bfloat16)
    send[:, width:] = raw_scores(pick, labels).astype(jnp.bfloat16)

    def rows(k, t):
        return pl.ds(pl.multiple_of(peers[k] * group + t * cap, cap), cap)

    def remote(src, dst, kind, k, device):
        return pltpu.make_async_remote_copy(
            src_ref=src,
            dst_ref=dst,
            send_sem=sems.at[kind, 0, k],
            recv_sem=sems.at[kind, 1, k],
            device_id=device,
            device_id_type=MESH,
        )

    order = [0, 1, 4, 2, 5, 3, 6, 7] if wide == 8 else list(range(wide))

    def chunk(k):
        return send.at[pl.ds(pl.multiple_of(peers[k] * cap, cap), cap)]

    routed = {k: remote(chunk(k), keys.at[rows(0, s)], 0, k, (peers[k], s)) for k in order[1:]}
    across = {
        k: remote(keys.at[rows(k, s)], keys.at[rows(k, s)], 1, k, (w, x_peer)) for k in order
    }
    beside = {
        k: remote(keys.at[rows(k, s)], keys.at[rows(k, s)], 2, k, (w, core_peer)) for k in order
    }
    onward = {
        k: remote(keys.at[rows(k, x_peer)], keys.at[rows(k, x_peer)], 3, k, (w, core_peer))
        for k in order
    }

    keys[rows(0, s), :] = send[pl.ds(pl.multiple_of(w * cap, cap), cap), :]
    pl.semaphore_wait(barrier, wide + 1)
    for k in order[1:]:
        routed[k].start()
    for at, k in enumerate(order):
        if k:
            routed[k].wait_recv()
        across[k].start()
        beside[k].start()
        if at:
            across[order[at - 1]].wait_recv()
            onward[order[at - 1]].start()
    across[order[-1]].wait_recv()
    onward[order[-1]].start()
    for k in order:
        beside[k].wait_recv()
        onward[k].wait_recv()

    queries = jnp.concatenate(
        [keys[pl.ds(pl.multiple_of(q * group + s * cap, cap), cap), :] for q in range(wide)], axis=0
    )
    lane = lax.broadcasted_iota(jnp.int32, (1, wide * cap), 1)
    query_place = lax.div(lane, cap) * group + s * cap + lax.rem(lane, cap)
    tile = 2 * group
    nearest = jnp.full((1, wide * cap), -1.0, jnp.float32)
    for first in range(0, wide * group, tile):
        scores = raw_scores(keys[first : first + tile, :width], queries[:, :width])
        same = raw_scores(keys[first : first + tile, width:], queries[:, width:])
        place = lax.broadcasted_iota(jnp.int32, (tile, 1), 0) + first
        allowed = (same > 0.5) & (place < query_place)
        nearest = jnp.maximum(
            nearest, jnp.max(jnp.where(allowed, scores, -1.0), axis=0, keepdims=True)
        )
    best[...] = nearest
    answers[w] = nearest
    backs = [
        pltpu.make_async_remote_copy(
            src_ref=best,
            dst_ref=answers.at[w],
            send_sem=back_sems.at[0, k],
            recv_sem=back_sems.at[1, k],
            device_id=(peers[k], s),
            device_id_type=MESH,
        )
        for k in range(1, wide)
    ]
    for copy in backs:
        copy.start()
    for copies in (routed, across, beside, onward):
        for copy in copies.values():
            copy.wait_send()
    for copy in backs:
        copy.wait()
    take = jnp.where(
        lax.broadcasted_iota(jnp.int32, (wide * cap, docs), 0) == w * cap + rank, 1.0, 0.0
    )
    found = jnp.dot(
        answers[:, 0, :], take, preferred_element_type=jnp.float32, precision=lax.Precision.HIGHEST
    )
    out_ref[...] = jnp.sum(jnp.where(own, found, 0.0), axis=0, keepdims=True)


def fused(embeddings, cluster_ids):
    docs, width = embeddings.shape
    wide = lax.axis_size("wide")
    cap = 2 * docs // wide
    out = pl.pallas_call(
        functools.partial(kernel, wide, cap),
        out_shape=jax.ShapeDtypeStruct((1, docs), jnp.float32),
        in_specs=[pl.BlockSpec(memory_space=pltpu.VMEM)] * 2,
        out_specs=pl.BlockSpec(memory_space=pltpu.VMEM),
        scratch_shapes=[
            pltpu.VMEM((wide * cap, width + META), jnp.bfloat16),
            pltpu.VMEM((4 * wide * cap, width + META), jnp.bfloat16),
            pltpu.VMEM((1, wide * cap), jnp.float32),
            pltpu.VMEM((wide, 1, wide * cap), jnp.float32),
            pltpu.SemaphoreType.DMA((4, 2, wide)),
            pltpu.SemaphoreType.DMA((2, wide)),
        ],
        compiler_params=pltpu.CompilerParams(
            collective_id=0, has_side_effects=True, vmem_limit_bytes=32 * 2**20
        ),
    )(embeddings, cluster_ids.reshape(1, docs))
    return out.reshape(docs)


def apply_mask(scores, query_meta, key_meta, along):
    allowed = (query_meta[0][:, None] == key_meta[0][None, :]) & (
        key_meta[1][None, :] < query_meta[1][:, None]
    )
    return jnp.max(jnp.where(allowed, scores, jnp.float32(-1.0)), axis=along)


def flatten_meta(meta):
    return (meta[:, 0, :].reshape(-1), meta[:, 1, :].reshape(-1))


def per_device(embeddings, cluster_ids):
    doc_count, width = embeddings.shape
    wide_count = lax.axis_size("wide")
    sub_count = lax.axis_size("sub")
    capacity = max(2, 2 * doc_count // wide_count)
    total_slots = wide_count * capacity
    values = embeddings.astype(jnp.float32)
    unit_rows = (
        values * lax.rsqrt(jnp.sum(values * values, axis=1, keepdims=True) + EPSILON)
    ).astype(jnp.bfloat16)
    owner_idx = cluster_ids // CL_DEV
    one_hot = (owner_idx[:, None] == jnp.arange(wide_count, dtype=jnp.int32)[None, :]).astype(
        jnp.int32
    )
    slot_rank = jnp.sum((jnp.cumsum(one_hot, axis=0) - one_hot) * one_hot, axis=1)
    slot_index = owner_idx * capacity + slot_rank
    device_row = lax.axis_index("wide") * sub_count + lax.axis_index("sub")
    positions = device_row * doc_count + jnp.arange(doc_count, dtype=jnp.int32)
    send_rows = jnp.zeros((total_slots, width), jnp.bfloat16).at[slot_index].set(unit_rows)
    send_rows = send_rows.reshape(wide_count, capacity, width)
    send_labels = jnp.full((total_slots,), -1, jnp.int32).at[slot_index].set(cluster_ids)
    send_places = jnp.full((total_slots,), -1, jnp.int32).at[slot_index].set(positions)
    send_meta = jnp.stack(
        [send_labels.reshape(wide_count, capacity), send_places.reshape(wide_count, capacity)],
        axis=1,
    )
    recv_rows, recv_meta = (
        lax.all_to_all(send_rows, "wide", split_axis=0, concat_axis=0, tiled=True),
        lax.all_to_all(send_meta, "wide", split_axis=0, concat_axis=0, tiled=True),
    )
    query_rows = recv_rows.reshape(-1, width)
    query_meta = flatten_meta(recv_meta)
    initial = jnp.full((total_slots,), -1.0, jnp.float32)
    key_rows = lax.all_gather(recv_rows, "sub", axis=0, tiled=True).reshape(-1, width)
    scores = raw_scores(query_rows, key_rows)
    nearest = jnp.maximum(
        initial,
        apply_mask(
            scores,
            query_meta,
            flatten_meta(lax.all_gather(recv_meta, "sub", axis=0, tiled=True)),
            1,
        ),
    )
    answer = lax.all_to_all(
        nearest.reshape(wide_count, capacity), "wide", split_axis=0, concat_axis=0, tiled=True
    )
    return answer.reshape(-1)[slot_index]


def solution(mesh):
    wide, sub = mesh.shape["wide"], mesh.shape["sub"]

    def step(embeddings, cluster_ids):
        cap = 2 * embeddings.shape[0] // wide
        if sub == 4 and wide & (wide - 1) == 0 and cap % 16 == 0:
            return fused(embeddings, cluster_ids)
        return per_device(embeddings, cluster_ids)

    return jax.shard_map(
        step,
        mesh=mesh,
        in_specs=(P(("wide", "sub"), None), P(("wide", "sub"))),
        out_specs=P(("wide", "sub")),
        check_vma=False,
    )
```

```python
import functools

import jax
import jax.numpy as jnp
from jax import lax
from jax.experimental import pallas as pl
from jax.experimental.pallas import tpu as pltpu
from jax.sharding import PartitionSpec as P

CL_DEV = 48
EPSILON = 1e-06
LABELS = 64
MESH = pl.DeviceIdType.MESH


def raw_scores(query_rows, key_rows):
    return lax.dot_general(
        query_rows, key_rows, (((1,), (1,)), ((), ())), preferred_element_type=jnp.float32
    )


def flip(index, mask, count):
    result, bit = 0, 1
    while bit < count:
        digit = lax.rem(lax.div(index, bit), 2)
        result = result + (1 - digit if mask & bit else digit) * bit
        bit *= 2
    return result


def kernel(wide, cap, emb_hbm, ids_hbm, out_ref, emb, ids_ref, send, keys, tags, labels, best, answers,
           in_sems, sems, tag_sems, tag_hops, back_sems):
    docs, width = emb.shape
    w, s = lax.axis_index("wide"), lax.axis_index("sub")
    group = 4 * cap
    half = wide // 2
    peers = {k: flip(w, k, wide) for k in range(wide)}
    x_peer, core_peer = flip(s, 2, 4), flip(s, 1, 4)

    barrier = pltpu.get_barrier_semaphore()
    for k in range(1, wide):
        pl.semaphore_signal(barrier, inc=1, device_id=(peers[k], s), device_id_type=MESH)
    for t in (x_peer, core_peer):
        pl.semaphore_signal(barrier, inc=1, device_id=(w, t), device_id_type=MESH)
    fetch_ids = pltpu.make_async_copy(ids_hbm, ids_ref, in_sems.at[0])
    fetch_emb = pltpu.make_async_copy(emb_hbm, emb, in_sems.at[1])
    fetch_ids.start()
    fetch_emb.start()
    fetch_ids.wait()

    ids = ids_ref[...]
    owner_row = lax.broadcasted_iota(jnp.int32, (wide, docs), 0)
    own = (ids >= owner_row * CL_DEV) & (ids < owner_row * CL_DEV + CL_DEV)
    ones = jnp.where(own, 1.0, 0.0)
    earlier = lax.broadcasted_iota(jnp.int32, (docs, docs), 0) < lax.broadcasted_iota(
        jnp.int32, (docs, docs), 1
    )
    ranks = jnp.dot(
        ones.astype(jnp.bfloat16),
        jnp.where(earlier, 1.0, 0.0).astype(jnp.bfloat16),
        preferred_element_type=jnp.float32,
    )
    rank = jnp.sum(ones * ranks, axis=0, keepdims=True).astype(jnp.int32)
    owner = jnp.sum(jnp.where(own, owner_row, 0), axis=0, keepdims=True)
    slot = owner * cap + rank
    label = jnp.where(own, (ids - owner_row * CL_DEV + 1).astype(jnp.float32), 0.0)
    lanes = lax.broadcasted_iota(jnp.int32, (group, docs), 0)
    for row, place in enumerate((s * cap + rank, lax.rem(w, 4) * cap + rank)):
        spread = jnp.where(lanes == place, 1.0, 0.0).astype(jnp.bfloat16)
        tags[:, row, :] = raw_scores(label.astype(jnp.bfloat16), spread)
    labels[s, w] = tags[w]
    pick = jnp.where(
        lax.broadcasted_iota(jnp.int32, (wide * cap, docs), 0) == slot, 1.0, 0.0
    ).astype(jnp.bfloat16)

    fetch_emb.wait()
    values = emb[...].astype(jnp.float32)
    unit = (
        values * lax.rsqrt(jnp.sum(values * values, axis=1, keepdims=True) + EPSILON)
    ).astype(jnp.bfloat16)
    send[...] = jnp.dot(pick, unit, preferred_element_type=jnp.float32).astype(jnp.bfloat16)

    def rows(k, t):
        return pl.ds(pl.multiple_of(peers[k] * group + t * cap, cap), cap)

    def copy_to(src, dst, send_sem, recv_sem, device):
        return pltpu.make_async_remote_copy(
            src_ref=src, dst_ref=dst, send_sem=send_sem, recv_sem=recv_sem,
            device_id=device, device_id_type=MESH,
        )

    def hop(kind, k, t, u):
        block = keys.at[rows(k, t)]
        return copy_to(block, block, sems.at[kind, 0, k], sems.at[kind, 1, k], (w, u))

    def tag_hop(kind, t, u):
        return copy_to(
            labels.at[t], labels.at[t], tag_hops.at[0, kind], tag_hops.at[1, kind], (w, u)
        )

    everyone = range(wide)
    others = range(1, wide)
    routed = {
        k: copy_to(
            send.at[pl.ds(pl.multiple_of(peers[k] * cap, cap), cap)], keys.at[rows(0, s)],
            sems.at[0, 0, k], sems.at[0, 1, k], (peers[k], s),
        )
        for k in others
    }
    tagged = {
        k: copy_to(
            tags.at[peers[k]], labels.at[s, w], tag_sems.at[0, k], tag_sems.at[1, k], (peers[k], s)
        )
        for k in others
    }
    across = {k: hop(1, k, s, x_peer) for k in everyone}
    beside = {k: hop(2, k, s, core_peer) for k in everyone}
    onward = {k: hop(3, k, x_peer, core_peer) for k in everyone}
    tag_across, tag_beside, tag_onward = (
        tag_hop(0, s, x_peer), tag_hop(1, s, core_peer), tag_hop(2, x_peer, core_peer)
    )

    def forward(k):
        across[k].start()
        beside[k].start()

    def relay(k):
        across[k].wait_recv()
        onward[k].start()

    def landed(k):
        beside[k].wait_recv()
        onward[k].wait_recv()

    query_lane = lax.broadcasted_iota(jnp.int32, (1, group), 1)

    def block(key_half, query_half):
        first = key_half * (half * group)
        queries = jnp.concatenate(
            [
                keys[pl.ds(pl.multiple_of((query_half * half + q) * group + s * cap, cap), cap), :]
                for q in range(half)
            ],
            axis=0,
        )
        kinds = lax.broadcasted_iota(jnp.int32, (LABELS, group), 0).astype(jnp.float32) + 1.0
        query_tag = labels[s, query_half * half, 1:2]
        for q in range(1, half):
            query_tag = jnp.maximum(query_tag, labels[s, query_half * half + q, 1:2])
        query_kind = jnp.where(kinds == query_tag, 1.0, 0.0).astype(jnp.bfloat16)
        query_place = (
            query_half * (half * group)
            + lax.div(query_lane, cap) * group + s * cap + lax.rem(query_lane, cap)
        )
        scores = raw_scores(
            keys[pl.ds(pl.multiple_of(first, group), half * group), :], queries
        )
        nearest = jnp.full((1, group), -1.0, jnp.float32)
        for q in range(half):
            key_tag = labels[0, key_half * half + q, 0:1]
            for t in range(1, 4):
                key_tag = jnp.maximum(key_tag, labels[t, key_half * half + q, 0:1])
            key_kind = jnp.where(kinds == key_tag, 1.0, 0.0).astype(jnp.bfloat16)
            same = lax.dot_general(
                key_kind, query_kind, (((0,), (0,)), ((), ())), preferred_element_type=jnp.float32
            )
            place = lax.broadcasted_iota(jnp.int32, (group, 1), 0) + (first + q * group)
            allowed = (same > 0.5) & (place < query_place)
            part = jnp.where(allowed, scores[q * group : (q + 1) * group], -1.0)
            nearest = jnp.maximum(nearest, jnp.max(part, axis=0, keepdims=True))
        return nearest

    keys[rows(0, s), :] = send[pl.ds(pl.multiple_of(w * cap, cap), cap), :]
    pl.semaphore_wait(barrier, wide + 1)
    near_half = lax.div(w, half)
    far_half = 1 - near_half
    for k in others:
        tagged[k].start()
    for k in (4, 1, 2, 3):
        routed[k].start()
    forward(0)
    routed[1].wait_recv()
    forward(1)
    routed[2].wait_recv()
    forward(2)
    routed[4].wait_send()
    routed[5].start()
    routed[3].wait_recv()
    forward(3)
    relay(0)
    routed[4].wait_recv()
    forward(4)
    for k in others:
        tagged[k].wait_recv()
    tag_across.start()
    tag_beside.start()
    relay(1)
    routed[5].wait_send()
    routed[6].start()
    relay(2)
    routed[5].wait_recv()
    forward(5)
    relay(3)
    tag_across.wait_recv()
    tag_onward.start()
    tag_beside.wait_recv()
    tag_onward.wait_recv()
    routed[6].wait_send()
    routed[7].start()
    for k in range(4):
        landed(k)
    best[near_half] = block(near_half, near_half)
    best[far_half] = jnp.full((1, group), -1.0, jnp.float32)
    relay(4)
    routed[6].wait_recv()
    forward(6)
    relay(5)
    routed[7].wait_recv()
    forward(7)
    relay(6)
    relay(7)
    for k in (1, 2, 3, 7):
        routed[k].wait_send()
    for k in range(4, 8):
        landed(k)
    across_best = block(0, 1)
    best[far_half] = jnp.maximum(best[far_half], block(far_half, far_half))
    best[1] = jnp.maximum(best[1], across_best)
    answers[w] = best[...]
    backs = [
        copy_to(best, answers.at[w], back_sems.at[0, k], back_sems.at[1, k], (peers[k], s))
        for k in others
    ]
    for copy in backs:
        copy.start()
    for copies in (tagged, across, beside, onward):
        for copy in copies.values():
            copy.wait_send()
    for copy in (tag_across, tag_beside, tag_onward):
        copy.wait_send()
    for copy in backs:
        copy.wait()
    mine = jnp.where(near_half == 0, answers[:, 0, 0, :], answers[:, 1, 0, :])
    take = jnp.where(lanes == lax.rem(w, half) * cap + rank, 1.0, 0.0)
    found = jnp.dot(
        mine, take, preferred_element_type=jnp.float32, precision=lax.Precision.HIGHEST
    )
    out_ref[...] = jnp.sum(jnp.where(own, found, 0.0), axis=0, keepdims=True)


def fused(embeddings, cluster_ids):
    docs, width = embeddings.shape
    wide = lax.axis_size("wide")
    cap = 2 * docs // wide
    slots = wide * cap
    out = pl.pallas_call(
        functools.partial(kernel, wide, cap),
        out_shape=jax.ShapeDtypeStruct((1, docs), jnp.float32),
        in_specs=[pl.BlockSpec(memory_space=pl.ANY)] * 2,
        out_specs=pl.BlockSpec(memory_space=pltpu.VMEM),
        scratch_shapes=[
            pltpu.VMEM((docs, width), jnp.bfloat16),
            pltpu.VMEM((1, docs), jnp.int32),
            pltpu.VMEM((slots, width), jnp.bfloat16),
            pltpu.VMEM((4 * slots, width), jnp.bfloat16),
            pltpu.VMEM((wide, 2, 4 * cap), jnp.float32),
            pltpu.VMEM((4, wide, 2, 4 * cap), jnp.float32),
            pltpu.VMEM((2, 1, 4 * cap), jnp.float32),
            pltpu.VMEM((wide, 2, 1, 4 * cap), jnp.float32),
            pltpu.SemaphoreType.DMA((2,)),
            pltpu.SemaphoreType.DMA((4, 2, wide)),
            pltpu.SemaphoreType.DMA((2, wide)),
            pltpu.SemaphoreType.DMA((2, 3)),
            pltpu.SemaphoreType.DMA((2, wide)),
        ],
        compiler_params=pltpu.CompilerParams(
            collective_id=0, has_side_effects=True, vmem_limit_bytes=32 * 2**20
        ),
    )(embeddings, cluster_ids.reshape(1, docs))
    return out.reshape(docs)


def apply_mask(scores, query_meta, key_meta, along):
    allowed = (query_meta[0][:, None] == key_meta[0][None, :]) & (
        key_meta[1][None, :] < query_meta[1][:, None]
    )
    return jnp.max(jnp.where(allowed, scores, jnp.float32(-1.0)), axis=along)


def flatten_meta(meta):
    return (meta[:, 0, :].reshape(-1), meta[:, 1, :].reshape(-1))


def per_device(embeddings, cluster_ids):
    doc_count, width = embeddings.shape
    wide_count = lax.axis_size("wide")
    sub_count = lax.axis_size("sub")
    capacity = max(2, 2 * doc_count // wide_count)
    total_slots = wide_count * capacity
    values = embeddings.astype(jnp.float32)
    unit_rows = (
        values * lax.rsqrt(jnp.sum(values * values, axis=1, keepdims=True) + EPSILON)
    ).astype(jnp.bfloat16)
    owner_idx = cluster_ids // CL_DEV
    one_hot = (owner_idx[:, None] == jnp.arange(wide_count, dtype=jnp.int32)[None, :]).astype(
        jnp.int32
    )
    slot_rank = jnp.sum((jnp.cumsum(one_hot, axis=0) - one_hot) * one_hot, axis=1)
    slot_index = owner_idx * capacity + slot_rank
    device_row = lax.axis_index("wide") * sub_count + lax.axis_index("sub")
    positions = device_row * doc_count + jnp.arange(doc_count, dtype=jnp.int32)
    send_rows = jnp.zeros((total_slots, width), jnp.bfloat16).at[slot_index].set(unit_rows)
    send_rows = send_rows.reshape(wide_count, capacity, width)
    send_labels = jnp.full((total_slots,), -1, jnp.int32).at[slot_index].set(cluster_ids)
    send_places = jnp.full((total_slots,), -1, jnp.int32).at[slot_index].set(positions)
    send_meta = jnp.stack(
        [send_labels.reshape(wide_count, capacity), send_places.reshape(wide_count, capacity)],
        axis=1,
    )
    recv_rows, recv_meta = (
        lax.all_to_all(send_rows, "wide", split_axis=0, concat_axis=0, tiled=True),
        lax.all_to_all(send_meta, "wide", split_axis=0, concat_axis=0, tiled=True),
    )
    query_rows = recv_rows.reshape(-1, width)
    query_meta = flatten_meta(recv_meta)
    initial = jnp.full((total_slots,), -1.0, jnp.float32)
    key_rows = lax.all_gather(recv_rows, "sub", axis=0, tiled=True).reshape(-1, width)
    scores = raw_scores(query_rows, key_rows)
    nearest = jnp.maximum(
        initial,
        apply_mask(
            scores,
            query_meta,
            flatten_meta(lax.all_gather(recv_meta, "sub", axis=0, tiled=True)),
            1,
        ),
    )
    answer = lax.all_to_all(
        nearest.reshape(wide_count, capacity), "wide", split_axis=0, concat_axis=0, tiled=True
    )
    return answer.reshape(-1)[slot_index]


def solution(mesh):
    wide, sub = mesh.shape["wide"], mesh.shape["sub"]

    def step(embeddings, cluster_ids):
        cap = 2 * embeddings.shape[0] // wide
        if (wide, sub, cap) == (8, 4, 32):
            return fused(embeddings, cluster_ids)
        return per_device(embeddings, cluster_ids)

    return jax.shard_map(
        step,
        mesh=mesh,
        in_specs=(P(("wide", "sub"), None), P(("wide", "sub"))),
        out_specs=P(("wide", "sub")),
        check_vma=False,
    )
```

```python
import functools

import jax
import jax.numpy as jnp
from jax import lax
from jax.experimental import pallas as pl
from jax.experimental.pallas import tpu as pltpu
from jax.sharding import PartitionSpec as P

CL_DEV = 48
EPSILON = 1e-06
LABELS = 64
MESH = pl.DeviceIdType.MESH


def raw_scores(query_rows, key_rows):
    return lax.dot_general(
        query_rows, key_rows, (((1,), (1,)), ((), ())), preferred_element_type=jnp.float32
    )


def flip(index, mask, count):
    result, bit = 0, 1
    while bit < count:
        digit = lax.rem(lax.div(index, bit), 2)
        result = result + (1 - digit if mask & bit else digit) * bit
        bit *= 2
    return result


def kernel(wide, cap, emb_hbm, ids_hbm, out_ref, emb, ids_ref, send, keys, tags, labels, best, answers,
           in_sems, sems, tag_sems, tag_hops, back_sems):
    docs, width = emb.shape
    w, s = lax.axis_index("wide"), lax.axis_index("sub")
    group = 4 * cap
    half = wide // 2
    peers = {k: flip(w, k, wide) for k in range(wide)}
    x_peer, core_peer = flip(s, 2, 4), flip(s, 1, 4)

    barrier = pltpu.get_barrier_semaphore()
    for k in range(1, wide):
        pl.semaphore_signal(barrier, inc=1, device_id=(peers[k], s), device_id_type=MESH)
    for t in (x_peer, core_peer):
        pl.semaphore_signal(barrier, inc=1, device_id=(w, t), device_id_type=MESH)
    fetch_ids = pltpu.make_async_copy(ids_hbm, ids_ref, in_sems.at[0])
    fetch_emb = pltpu.make_async_copy(emb_hbm, emb, in_sems.at[1])
    fetch_ids.start()
    fetch_emb.start()
    fetch_ids.wait()

    ids = ids_ref[...]
    owner_row = lax.broadcasted_iota(jnp.int32, (wide, docs), 0)
    own = (ids >= owner_row * CL_DEV) & (ids < owner_row * CL_DEV + CL_DEV)
    ones = jnp.where(own, 1.0, 0.0)
    earlier = lax.broadcasted_iota(jnp.int32, (docs, docs), 0) < lax.broadcasted_iota(
        jnp.int32, (docs, docs), 1
    )
    ranks = jnp.dot(
        ones.astype(jnp.bfloat16),
        jnp.where(earlier, 1.0, 0.0).astype(jnp.bfloat16),
        preferred_element_type=jnp.float32,
    )
    rank = jnp.sum(ones * ranks, axis=0, keepdims=True).astype(jnp.int32)
    owner = jnp.sum(jnp.where(own, owner_row, 0), axis=0, keepdims=True)
    slot = owner * cap + rank
    label = jnp.where(own, (ids - owner_row * CL_DEV + 1).astype(jnp.float32), 0.0)
    lanes = lax.broadcasted_iota(jnp.int32, (group, docs), 0)
    for row, place in enumerate((s * cap + rank, lax.rem(w, 4) * cap + rank)):
        spread = jnp.where(lanes == place, 1.0, 0.0).astype(jnp.bfloat16)
        tags[:, row, :] = raw_scores(label.astype(jnp.bfloat16), spread)
    labels[s, w] = tags[w]
    pick = jnp.where(
        lax.broadcasted_iota(jnp.int32, (wide * cap, docs), 0) == slot, 1.0, 0.0
    ).astype(jnp.bfloat16)

    fetch_emb.wait()
    values = emb[...].astype(jnp.float32)
    unit = (
        values * lax.rsqrt(jnp.sum(values * values, axis=1, keepdims=True) + EPSILON)
    ).astype(jnp.bfloat16)
    send[...] = jnp.dot(pick, unit, preferred_element_type=jnp.float32).astype(jnp.bfloat16)

    def rows(k, t):
        return pl.ds(pl.multiple_of(peers[k] * group + t * cap, cap), cap)

    def copy_to(src, dst, send_sem, recv_sem, device):
        return pltpu.make_async_remote_copy(
            src_ref=src, dst_ref=dst, send_sem=send_sem, recv_sem=recv_sem,
            device_id=device, device_id_type=MESH,
        )

    def hop(kind, k, t, u):
        block = keys.at[rows(k, t)]
        return copy_to(block, block, sems.at[kind, 0, k], sems.at[kind, 1, k], (w, u))

    def tag_hop(kind, t, u):
        return copy_to(
            labels.at[t], labels.at[t], tag_hops.at[0, kind], tag_hops.at[1, kind], (w, u)
        )

    everyone = range(wide)
    others = range(1, wide)
    routed = {
        k: copy_to(
            send.at[pl.ds(pl.multiple_of(peers[k] * cap, cap), cap)], keys.at[rows(0, s)],
            sems.at[0, 0, k], sems.at[0, 1, k], (peers[k], s),
        )
        for k in others
    }
    tagged = {
        k: copy_to(
            tags.at[peers[k]], labels.at[s, w], tag_sems.at[0, k], tag_sems.at[1, k], (peers[k], s)
        )
        for k in others
    }
    across = {k: hop(1, k, s, x_peer) for k in everyone}
    beside = {k: hop(2, k, s, core_peer) for k in everyone}
    onward = {k: hop(3, k, x_peer, core_peer) for k in everyone}
    tag_across, tag_beside, tag_onward = (
        tag_hop(0, s, x_peer), tag_hop(1, s, core_peer), tag_hop(2, x_peer, core_peer)
    )

    def forward(k):
        across[k].start()
        beside[k].start()

    def relay(k):
        across[k].wait_recv()
        onward[k].start()

    def landed(k):
        beside[k].wait_recv()
        onward[k].wait_recv()

    query_lane = lax.broadcasted_iota(jnp.int32, (1, group), 1)

    def block(key_half, query_half):
        first = key_half * (half * group)
        queries = jnp.concatenate(
            [
                keys[pl.ds(pl.multiple_of((query_half * half + q) * group + s * cap, cap), cap), :]
                for q in range(half)
            ],
            axis=0,
        )
        kinds = lax.broadcasted_iota(jnp.int32, (LABELS, group), 0).astype(jnp.float32) + 1.0
        query_tag = labels[s, query_half * half, 1:2]
        for q in range(1, half):
            query_tag = jnp.maximum(query_tag, labels[s, query_half * half + q, 1:2])
        query_kind = jnp.where(kinds == query_tag, 1.0, 0.0).astype(jnp.bfloat16)
        query_place = (
            query_half * (half * group)
            + lax.div(query_lane, cap) * group + s * cap + lax.rem(query_lane, cap)
        )
        scores = raw_scores(
            keys[pl.ds(pl.multiple_of(first, group), half * group), :], queries
        )
        nearest = jnp.full((1, group), -1.0, jnp.float32)
        for q in range(half):
            key_tag = labels[0, key_half * half + q, 0:1]
            for t in range(1, 4):
                key_tag = jnp.maximum(key_tag, labels[t, key_half * half + q, 0:1])
            key_kind = jnp.where(kinds == key_tag, 1.0, 0.0).astype(jnp.bfloat16)
            same = lax.dot_general(
                key_kind, query_kind, (((0,), (0,)), ((), ())), preferred_element_type=jnp.float32
            )
            place = lax.broadcasted_iota(jnp.int32, (group, 1), 0) + (first + q * group)
            allowed = (same > 0.5) & (place < query_place)
            part = jnp.where(allowed, scores[q * group : (q + 1) * group], -1.0)
            nearest = jnp.maximum(nearest, jnp.max(part, axis=0, keepdims=True))
        return nearest

    keys[rows(0, s), :] = send[pl.ds(pl.multiple_of(w * cap, cap), cap), :]
    pl.semaphore_wait(barrier, wide + 1)
    near_half = lax.div(w, half)
    far_half = 1 - near_half
    for k in (4, 1, 2, 3, 5):
        routed[k].start()
    for k in others:
        tagged[k].start()
    forward(0)
    for k in (1, 2, 3):
        routed[k].wait_recv()
        forward(k)
    routed[4].wait_send()
    routed[6].start()
    routed[4].wait_recv()
    forward(4)
    routed[5].wait_send()
    routed[7].start()
    routed[5].wait_recv()
    forward(5)
    for k in others:
        tagged[k].wait_recv()
    tag_across.start()
    tag_beside.start()
    for k in range(4):
        relay(k)
    tag_across.wait_recv()
    tag_onward.start()
    tag_beside.wait_recv()
    tag_onward.wait_recv()
    for k in range(4):
        landed(k)
    best[near_half] = block(near_half, near_half)
    best[far_half] = jnp.full((1, group), -1.0, jnp.float32)
    routed[6].wait_recv()
    forward(6)
    relay(4)
    routed[7].wait_recv()
    forward(7)
    for k in (5, 6, 7):
        relay(k)
    for k in (1, 2, 3, 6, 7):
        routed[k].wait_send()
    for k in range(4, 8):
        landed(k)
    across_best = block(0, 1)
    best[far_half] = jnp.maximum(best[far_half], block(far_half, far_half))
    best[1] = jnp.maximum(best[1], across_best)
    answers[w] = best[...]
    backs = [
        copy_to(best, answers.at[w], back_sems.at[0, k], back_sems.at[1, k], (peers[k], s))
        for k in others
    ]
    for copy in backs:
        copy.start()
    for copies in (tagged, across, beside, onward):
        for copy in copies.values():
            copy.wait_send()
    for copy in (tag_across, tag_beside, tag_onward):
        copy.wait_send()
    for copy in backs:
        copy.wait()
    mine = jnp.where(near_half == 0, answers[:, 0, 0, :], answers[:, 1, 0, :])
    take = jnp.where(lanes == lax.rem(w, half) * cap + rank, 1.0, 0.0)
    found = jnp.dot(
        mine, take, preferred_element_type=jnp.float32, precision=lax.Precision.HIGHEST
    )
    out_ref[...] = jnp.sum(jnp.where(own, found, 0.0), axis=0, keepdims=True)


def fused(embeddings, cluster_ids):
    docs, width = embeddings.shape
    wide = lax.axis_size("wide")
    cap = 2 * docs // wide
    slots = wide * cap
    out = pl.pallas_call(
        functools.partial(kernel, wide, cap),
        out_shape=jax.ShapeDtypeStruct((1, docs), jnp.float32),
        in_specs=[pl.BlockSpec(memory_space=pltpu.HBM)] * 2,
        out_specs=pl.BlockSpec(memory_space=pltpu.VMEM),
        scratch_shapes=[
            pltpu.VMEM((docs, width), jnp.bfloat16),
            pltpu.VMEM((1, docs), jnp.int32),
            pltpu.VMEM((slots, width), jnp.bfloat16),
            pltpu.VMEM((4 * slots, width), jnp.bfloat16),
            pltpu.VMEM((wide, 2, 4 * cap), jnp.float32),
            pltpu.VMEM((4, wide, 2, 4 * cap), jnp.float32),
            pltpu.VMEM((2, 1, 4 * cap), jnp.float32),
            pltpu.VMEM((wide, 2, 1, 4 * cap), jnp.float32),
            pltpu.SemaphoreType.DMA((2,)),
            pltpu.SemaphoreType.DMA((4, 2, wide)),
            pltpu.SemaphoreType.DMA((2, wide)),
            pltpu.SemaphoreType.DMA((2, 3)),
            pltpu.SemaphoreType.DMA((2, wide)),
        ],
        compiler_params=pltpu.CompilerParams(
            collective_id=0, has_side_effects=True, vmem_limit_bytes=32 * 2**20
        ),
    )(embeddings, cluster_ids.reshape(1, docs))
    return out.reshape(docs)


def apply_mask(scores, query_meta, key_meta, along):
    allowed = (query_meta[0][:, None] == key_meta[0][None, :]) & (
        key_meta[1][None, :] < query_meta[1][:, None]
    )
    return jnp.max(jnp.where(allowed, scores, jnp.float32(-1.0)), axis=along)


def flatten_meta(meta):
    return (meta[:, 0, :].reshape(-1), meta[:, 1, :].reshape(-1))


def per_device(embeddings, cluster_ids):
    doc_count, width = embeddings.shape
    wide_count = lax.axis_size("wide")
    sub_count = lax.axis_size("sub")
    capacity = max(2, 2 * doc_count // wide_count)
    total_slots = wide_count * capacity
    values = embeddings.astype(jnp.float32)
    unit_rows = (
        values * lax.rsqrt(jnp.sum(values * values, axis=1, keepdims=True) + EPSILON)
    ).astype(jnp.bfloat16)
    owner_idx = cluster_ids // CL_DEV
    one_hot = (owner_idx[:, None] == jnp.arange(wide_count, dtype=jnp.int32)[None, :]).astype(
        jnp.int32
    )
    slot_rank = jnp.sum((jnp.cumsum(one_hot, axis=0) - one_hot) * one_hot, axis=1)
    slot_index = owner_idx * capacity + slot_rank
    device_row = lax.axis_index("wide") * sub_count + lax.axis_index("sub")
    positions = device_row * doc_count + jnp.arange(doc_count, dtype=jnp.int32)
    send_rows = jnp.zeros((total_slots, width), jnp.bfloat16).at[slot_index].set(unit_rows)
    send_rows = send_rows.reshape(wide_count, capacity, width)
    send_labels = jnp.full((total_slots,), -1, jnp.int32).at[slot_index].set(cluster_ids)
    send_places = jnp.full((total_slots,), -1, jnp.int32).at[slot_index].set(positions)
    send_meta = jnp.stack(
        [send_labels.reshape(wide_count, capacity), send_places.reshape(wide_count, capacity)],
        axis=1,
    )
    recv_rows, recv_meta = (
        lax.all_to_all(send_rows, "wide", split_axis=0, concat_axis=0, tiled=True),
        lax.all_to_all(send_meta, "wide", split_axis=0, concat_axis=0, tiled=True),
    )
    query_rows = recv_rows.reshape(-1, width)
    query_meta = flatten_meta(recv_meta)
    initial = jnp.full((total_slots,), -1.0, jnp.float32)
    key_rows = lax.all_gather(recv_rows, "sub", axis=0, tiled=True).reshape(-1, width)
    scores = raw_scores(query_rows, key_rows)
    nearest = jnp.maximum(
        initial,
        apply_mask(
            scores,
            query_meta,
            flatten_meta(lax.all_gather(recv_meta, "sub", axis=0, tiled=True)),
            1,
        ),
    )
    answer = lax.all_to_all(
        nearest.reshape(wide_count, capacity), "wide", split_axis=0, concat_axis=0, tiled=True
    )
    return answer.reshape(-1)[slot_index]


def solution(mesh):
    wide, sub = mesh.shape["wide"], mesh.shape["sub"]

    def step(embeddings, cluster_ids):
        cap = 2 * embeddings.shape[0] // wide
        if (wide, sub, cap) == (8, 4, 32):
            return fused(embeddings, cluster_ids)
        return per_device(embeddings, cluster_ids)

    return jax.shard_map(
        step,
        mesh=mesh,
        in_specs=(P(("wide", "sub"), None), P(("wide", "sub"))),
        out_specs=P(("wide", "sub")),
        check_vma=False,
    )
```

```python
import functools

import jax
import jax.numpy as jnp
from jax import lax
from jax.experimental import pallas as pl
from jax.experimental.pallas import tpu as pltpu
from jax.sharding import PartitionSpec as P

CL_DEV = 48
EPSILON = 1e-06
LABELS = 64
MESH = pl.DeviceIdType.MESH


def raw_scores(query_rows, key_rows):
    return lax.dot_general(
        query_rows, key_rows, (((1,), (1,)), ((), ())), preferred_element_type=jnp.float32
    )


def flip(index, mask, count):
    result, bit = 0, 1
    while bit < count:
        digit = lax.rem(lax.div(index, bit), 2)
        result = result + (1 - digit if mask & bit else digit) * bit
        bit *= 2
    return result


def kernel(wide, cap, emb_hbm, ids_hbm, out_ref, emb, ids_ref, send, keys, tags, labels, best, answers,
           in_sems, sems, tag_sems, tag_hops, back_sems):
    docs, width = emb.shape
    w, s = lax.axis_index("wide"), lax.axis_index("sub")
    group = 4 * cap
    half = wide // 2
    peers = {k: flip(w, k, wide) for k in range(wide)}
    x_peer, core_peer = flip(s, 2, 4), flip(s, 1, 4)

    barrier = pltpu.get_barrier_semaphore()
    for k in range(1, wide):
        pl.semaphore_signal(barrier, inc=1, device_id=(peers[k], s), device_id_type=MESH)
    for t in (x_peer, core_peer):
        pl.semaphore_signal(barrier, inc=1, device_id=(w, t), device_id_type=MESH)
    fetch_ids = pltpu.make_async_copy(ids_hbm, ids_ref, in_sems.at[0])
    fetch_emb = pltpu.make_async_copy(emb_hbm, emb, in_sems.at[1])
    fetch_ids.start()
    fetch_emb.start()
    fetch_ids.wait()

    ids = ids_ref[...]
    owner_row = lax.broadcasted_iota(jnp.int32, (wide, docs), 0)
    own = (ids >= owner_row * CL_DEV) & (ids < owner_row * CL_DEV + CL_DEV)
    ones = jnp.where(own, 1.0, 0.0)
    earlier = lax.broadcasted_iota(jnp.int32, (docs, docs), 0) < lax.broadcasted_iota(
        jnp.int32, (docs, docs), 1
    )
    ranks = jnp.dot(
        ones.astype(jnp.bfloat16),
        jnp.where(earlier, 1.0, 0.0).astype(jnp.bfloat16),
        preferred_element_type=jnp.float32,
    )
    rank = jnp.sum(ones * ranks, axis=0, keepdims=True).astype(jnp.int32)
    owner = jnp.sum(jnp.where(own, owner_row, 0), axis=0, keepdims=True)
    slot = owner * cap + rank
    label = jnp.where(own, (ids - owner_row * CL_DEV + 1).astype(jnp.float32), 0.0)
    lanes = lax.broadcasted_iota(jnp.int32, (group, docs), 0)
    for row, place in enumerate((s * cap + rank, lax.rem(w, 4) * cap + rank)):
        spread = jnp.where(lanes == place, 1.0, 0.0).astype(jnp.bfloat16)
        tags[:, row, :] = raw_scores(label.astype(jnp.bfloat16), spread)
    labels[s, w] = tags[w]
    pick = jnp.where(
        lax.broadcasted_iota(jnp.int32, (wide * cap, docs), 0) == slot, 1.0, 0.0
    ).astype(jnp.bfloat16)

    fetch_emb.wait()
    values = emb[...].astype(jnp.float32)
    unit = (
        values * lax.rsqrt(jnp.sum(values * values, axis=1, keepdims=True) + EPSILON)
    ).astype(jnp.bfloat16)
    send[...] = jnp.dot(pick, unit, preferred_element_type=jnp.float32).astype(jnp.bfloat16)

    def rows(k, t):
        return pl.ds(pl.multiple_of(peers[k] * group + t * cap, cap), cap)

    def copy_to(src, dst, send_sem, recv_sem, device):
        return pltpu.make_async_remote_copy(
            src_ref=src, dst_ref=dst, send_sem=send_sem, recv_sem=recv_sem,
            device_id=device, device_id_type=MESH,
        )

    def hop(kind, k, t, u):
        block = keys.at[rows(k, t)]
        return copy_to(block, block, sems.at[kind, 0, k], sems.at[kind, 1, k], (w, u))

    def tag_hop(kind, t, u):
        return copy_to(
            labels.at[t], labels.at[t], tag_hops.at[0, kind], tag_hops.at[1, kind], (w, u)
        )

    everyone = range(wide)
    others = range(1, wide)
    routed = {
        k: copy_to(
            send.at[pl.ds(pl.multiple_of(peers[k] * cap, cap), cap)], keys.at[rows(0, s)],
            sems.at[0, 0, k], sems.at[0, 1, k], (peers[k], s),
        )
        for k in others
    }
    tagged = {
        k: copy_to(
            tags.at[peers[k]], labels.at[s, w], tag_sems.at[0, k], tag_sems.at[1, k], (peers[k], s)
        )
        for k in others
    }
    across = {k: hop(1, k, s, x_peer) for k in everyone}
    beside = {k: hop(2, k, s, core_peer) for k in everyone}
    onward = {k: hop(3, k, x_peer, core_peer) for k in everyone}
    tag_across, tag_beside, tag_onward = (
        tag_hop(0, s, x_peer), tag_hop(1, s, core_peer), tag_hop(2, x_peer, core_peer)
    )

    def forward(k):
        across[k].start()
        beside[k].start()

    def relay(k):
        across[k].wait_recv()
        onward[k].start()

    def landed(k):
        beside[k].wait_recv()
        onward[k].wait_recv()

    def block(key_first, key_count, query_first, query_count):
        lanes_here = query_count * cap
        queries = jnp.concatenate(
            [
                keys[pl.ds(pl.multiple_of((query_first + q) * group + s * cap, cap), cap), :]
                for q in range(query_count)
            ],
            axis=0,
        )
        kinds = lax.broadcasted_iota(jnp.int32, (LABELS, group), 0).astype(jnp.float32) + 1.0
        query_kinds = []
        for base in range(0, query_count, 4):
            query_tag = labels[s, query_first + base, 1:2]
            for q in range(1, 4):
                query_tag = jnp.maximum(query_tag, labels[s, query_first + base + q, 1:2])
            query_kinds.append(jnp.where(kinds == query_tag, 1.0, 0.0).astype(jnp.bfloat16))
        query_kind = jnp.concatenate(query_kinds, axis=1)
        query_lane = lax.broadcasted_iota(jnp.int32, (1, lanes_here), 1)
        query_place = (
            query_first * group + lax.div(query_lane, cap) * group + s * cap
            + lax.rem(query_lane, cap)
        )
        first = key_first * group
        scores = raw_scores(
            keys[pl.ds(pl.multiple_of(first, group), key_count * group), :], queries
        )
        nearest = jnp.full((1, lanes_here), -1.0, jnp.float32)
        for q in range(key_count):
            key_tag = labels[0, key_first + q, 0:1]
            for t in range(1, 4):
                key_tag = jnp.maximum(key_tag, labels[t, key_first + q, 0:1])
            key_kind = jnp.where(kinds == key_tag, 1.0, 0.0).astype(jnp.bfloat16)
            same = lax.dot_general(
                key_kind, query_kind, (((0,), (0,)), ((), ())), preferred_element_type=jnp.float32
            )
            place = lax.broadcasted_iota(jnp.int32, (group, 1), 0) + (first + q * group)
            allowed = (same > 0.5) & (place < query_place)
            part = jnp.where(allowed, scores[q * group : (q + 1) * group], -1.0)
            nearest = jnp.maximum(nearest, jnp.max(part, axis=0, keepdims=True))
        return nearest

    keys[rows(0, s), :] = send[pl.ds(pl.multiple_of(w * cap, cap), cap), :]
    pl.semaphore_wait(barrier, wide + 1)
    near_half = lax.div(w, half)
    far_half = 1 - near_half
    pairs = [lax.div(peers[k], 2) * 2 for k in (4, 6)]
    for k in (4, 1, 2, 3, 5):
        routed[k].start()
    for k in others:
        tagged[k].start()
    forward(0)
    for k in (1, 2, 3):
        routed[k].wait_recv()
        forward(k)
    routed[4].wait_send()
    routed[6].start()
    routed[4].wait_recv()
    forward(4)
    routed[5].wait_send()
    routed[7].start()
    routed[5].wait_recv()
    forward(5)
    for k in others:
        tagged[k].wait_recv()
    tag_across.start()
    tag_beside.start()
    for k in range(4):
        relay(k)
    tag_across.wait_recv()
    tag_onward.start()
    tag_beside.wait_recv()
    tag_onward.wait_recv()
    for k in range(4):
        landed(k)
    best[near_half] = block(near_half * half, half, near_half * half, half)
    routed[6].wait_recv()
    forward(6)
    relay(4)
    routed[7].wait_recv()
    forward(7)
    relay(5)
    best[far_half] = block(near_half * half, half, far_half * half, half)
    relay(6)
    landed(4)
    landed(5)
    nearest = block(pairs[0], 2, 0, wide)
    relay(7)
    landed(6)
    landed(7)
    nearest = jnp.maximum(nearest, block(pairs[1], 2, 0, wide))
    best[0] = jnp.maximum(best[0], nearest[:, :group])
    best[1] = jnp.maximum(best[1], nearest[:, group:])
    for k in (1, 2, 3, 6, 7):
        routed[k].wait_send()
    answers[w] = best[...]
    backs = [
        copy_to(best, answers.at[w], back_sems.at[0, k], back_sems.at[1, k], (peers[k], s))
        for k in others
    ]
    for copy in backs:
        copy.start()
    for copies in (tagged, across, beside, onward):
        for copy in copies.values():
            copy.wait_send()
    for copy in (tag_across, tag_beside, tag_onward):
        copy.wait_send()
    for copy in backs:
        copy.wait()
    mine = jnp.where(near_half == 0, answers[:, 0, 0, :], answers[:, 1, 0, :])
    take = jnp.where(lanes == lax.rem(w, half) * cap + rank, 1.0, 0.0)
    found = jnp.dot(
        mine, take, preferred_element_type=jnp.float32, precision=lax.Precision.HIGHEST
    )
    out_ref[...] = jnp.sum(jnp.where(own, found, 0.0), axis=0, keepdims=True)


def fused(embeddings, cluster_ids):
    docs, width = embeddings.shape
    wide = lax.axis_size("wide")
    cap = 2 * docs // wide
    slots = wide * cap
    out = pl.pallas_call(
        functools.partial(kernel, wide, cap),
        out_shape=jax.ShapeDtypeStruct((1, docs), jnp.float32),
        in_specs=[pl.BlockSpec(memory_space=pl.ANY)] * 2,
        out_specs=pl.BlockSpec(memory_space=pltpu.VMEM),
        scratch_shapes=[
            pltpu.VMEM((docs, width), jnp.bfloat16),
            pltpu.VMEM((1, docs), jnp.int32),
            pltpu.VMEM((slots, width), jnp.bfloat16),
            pltpu.VMEM((4 * slots, width), jnp.bfloat16),
            pltpu.VMEM((wide, 2, 4 * cap), jnp.float32),
            pltpu.VMEM((4, wide, 2, 4 * cap), jnp.float32),
            pltpu.VMEM((2, 1, 4 * cap), jnp.float32),
            pltpu.VMEM((wide, 2, 1, 4 * cap), jnp.float32),
            pltpu.SemaphoreType.DMA((2,)),
            pltpu.SemaphoreType.DMA((4, 2, wide)),
            pltpu.SemaphoreType.DMA((2, wide)),
            pltpu.SemaphoreType.DMA((2, 3)),
            pltpu.SemaphoreType.DMA((2, wide)),
        ],
        compiler_params=pltpu.CompilerParams(
            collective_id=0, has_side_effects=True
        ),
    )(embeddings, cluster_ids.reshape(1, docs))
    return out.reshape(docs)


def apply_mask(scores, query_meta, key_meta, along):
    allowed = (query_meta[0][:, None] == key_meta[0][None, :]) & (
        key_meta[1][None, :] < query_meta[1][:, None]
    )
    return jnp.max(jnp.where(allowed, scores, jnp.float32(-1.0)), axis=along)


def flatten_meta(meta):
    return (meta[:, 0, :].reshape(-1), meta[:, 1, :].reshape(-1))


def per_device(embeddings, cluster_ids):
    doc_count, width = embeddings.shape
    wide_count = lax.axis_size("wide")
    sub_count = lax.axis_size("sub")
    capacity = max(2, 2 * doc_count // wide_count)
    total_slots = wide_count * capacity
    values = embeddings.astype(jnp.float32)
    unit_rows = (
        values * lax.rsqrt(jnp.sum(values * values, axis=1, keepdims=True) + EPSILON)
    ).astype(jnp.bfloat16)
    owner_idx = cluster_ids // CL_DEV
    one_hot = (owner_idx[:, None] == jnp.arange(wide_count, dtype=jnp.int32)[None, :]).astype(
        jnp.int32
    )
    slot_rank = jnp.sum((jnp.cumsum(one_hot, axis=0) - one_hot) * one_hot, axis=1)
    slot_index = owner_idx * capacity + slot_rank
    device_row = lax.axis_index("wide") * sub_count + lax.axis_index("sub")
    positions = device_row * doc_count + jnp.arange(doc_count, dtype=jnp.int32)
    send_rows = jnp.zeros((total_slots, width), jnp.bfloat16).at[slot_index].set(unit_rows)
    send_rows = send_rows.reshape(wide_count, capacity, width)
    send_labels = jnp.full((total_slots,), -1, jnp.int32).at[slot_index].set(cluster_ids)
    send_places = jnp.full((total_slots,), -1, jnp.int32).at[slot_index].set(positions)
    send_meta = jnp.stack(
        [send_labels.reshape(wide_count, capacity), send_places.reshape(wide_count, capacity)],
        axis=1,
    )
    recv_rows, recv_meta = (
        lax.all_to_all(send_rows, "wide", split_axis=0, concat_axis=0, tiled=True),
        lax.all_to_all(send_meta, "wide", split_axis=0, concat_axis=0, tiled=True),
    )
    query_rows = recv_rows.reshape(-1, width)
    query_meta = flatten_meta(recv_meta)
    initial = jnp.full((total_slots,), -1.0, jnp.float32)
    key_rows = lax.all_gather(recv_rows, "sub", axis=0, tiled=True).reshape(-1, width)
    scores = raw_scores(query_rows, key_rows)
    nearest = jnp.maximum(
        initial,
        apply_mask(
            scores,
            query_meta,
            flatten_meta(lax.all_gather(recv_meta, "sub", axis=0, tiled=True)),
            1,
        ),
    )
    answer = lax.all_to_all(
        nearest.reshape(wide_count, capacity), "wide", split_axis=0, concat_axis=0, tiled=True
    )
    return answer.reshape(-1)[slot_index]


def solution(mesh):
    wide, sub = mesh.shape["wide"], mesh.shape["sub"]

    def step(embeddings, cluster_ids):
        cap = 2 * embeddings.shape[0] // wide
        if (wide, sub, cap) == (8, 4, 32):
            return fused(embeddings, cluster_ids)
        return per_device(embeddings, cluster_ids)

    return jax.shard_map(
        step,
        mesh=mesh,
        in_specs=(P(("wide", "sub"), None), P(("wide", "sub"))),
        out_specs=P(("wide", "sub")),
        check_vma=False,
    )
```
